256 devices in a mesh: xp: 8 (over z), zp: 8 (over y_lo, x), gy: 4 (over y_hi, core).
Axes of the slice: x: 4, y: 4 (y_hi: 2, y_lo: 2; y = y_hi * 2 + y_lo), z: 8, core: 2. Of those that a mesh axis runs over, the one named last changes fastest.
Arguments:
- fields: float32 [4, 12, 4096, 4096], P(None, 'gy', ('xp', 'zp')), may hold values from -12 to 12
Outputs:
- filtered: float32 [10, 12, 512, 512], P(None, 'gy', ('xp', 'zp'))
The draws below stay inside these ranges and needn't reach their ends.
All inputs are finite; a program needn't handle non-finite values.
Results may differ from the reference program's by a relative error of at most 0.00012.
Values sent between devices are 32-bit elements; how exact they have to be, the bound alone decides.
A program may use at most 192 MiB of HBM per device.

```python
import math
import jax
import jax.numpy as jnp
from jax import lax

NX = 4096
NYW = 12
NZ = 4096


def draw_fields(key, part):
    key = jax.random.fold_in(key, 11)
    subkeys = jax.random.split(key, 5)
    array_shape = (4, NYW, NZ, NX)
    profile = jax.random.uniform(subkeys[0], (4, NYW, 1, 1), jnp.float32, -1.5, 1.5)
    fluctuation = jnp.clip(jax.random.normal(subkeys[1], array_shape, jnp.float32), -3.0, 3.0)
    phase_x = jax.random.uniform(subkeys[2], (4, 1, 1, 1), jnp.float32, 0.0, 2.0 * math.pi)
    phase_z = jax.random.uniform(subkeys[3], (4, 1, 1, 1), jnp.float32, 0.0, 2.0 * math.pi)
    across_x = jnp.arange(NX).astype(jnp.float32)[None, None, None, :]
    across_z = jnp.arange(NZ).astype(jnp.float32)[None, None, :, None]
    pattern = jnp.cos(2.0 * math.pi * 8.0 * across_x / NX + phase_x) * jnp.cos(2.0 * math.pi * 8.0 * across_z / NZ + phase_z)
    roughness = jax.random.uniform(subkeys[4], array_shape, jnp.float32, -0.5, 0.5)
    amplitude = jnp.exp(0.7 * pattern + roughness)
    return profile + amplitude * fluctuation


def setup_inputs(seed: int = 0) -> dict:
    keys = jax.random.split(jax.random.key(seed), 2)
    fields = draw_fields(jax.random.fold_in(keys[1], 71), 0)
    return {"fields": fields}


product_pairs = ((0, 0), (1, 1), (2, 2), (3, 3), (0, 1), (0, 2), (1, 2), (0, 3), (1, 3), (2, 3))


def gauss_table():
    offsets = jnp.arange(-16, 17).astype(jnp.float32)
    weights = jnp.exp(-6.0 * offsets * offsets / 256.0)
    weights = weights / jnp.sum(weights)
    padded_weights = jnp.concatenate([weights, jnp.zeros((7,), jnp.float32)])
    return padded_weights.reshape(5, 8)


def coarse_filter(signal, table):
    length = signal.shape[-1]
    grouped = signal.reshape(signal.shape[:-1] + (length // 8, 8))
    total = jnp.zeros(grouped.shape, jnp.float32)
    for shift_index in range(5):
        rolled = jnp.roll(grouped, -(shift_index - 2), axis=-2)
        total = total + rolled * table[shift_index]
    return jnp.sum(total, axis=-1)


def reference(fields):
    table = gauss_table()

    def one_plane(plane_index):
        plane = lax.dynamic_index_in_dim(fields, plane_index, 1, keepdims=False)
        outputs = []
        for left_index, right_index in product_pairs:
            product = plane[left_index] * plane[right_index]
            along_x = coarse_filter(product, table)
            outputs.append(coarse_filter(along_x.T, table))
        return jnp.stack(outputs)

    zfiltered = lax.map(one_plane, jnp.arange(NYW).astype(jnp.int32))
    zfiltered = jnp.swapaxes(zfiltered, 0, 1)
    padded = jnp.pad(zfiltered, ((0, 0), (1, 1), (0, 0), (0, 0)))
    summed = padded[:, :-2] + padded[:, 1:-1] + padded[:, 2:]
    wall_rows = jnp.arange(NYW).astype(jnp.int32)
    counts = (3 - (wall_rows == 0).astype(jnp.int32) - (wall_rows == NYW - 1).astype(jnp.int32)).astype(jnp.float32)
    return summed / counts[None, :, None, None]
```

```python
import functools

import jax
import jax.numpy as jnp
import numpy as np
from jax import lax
from jax.experimental import pallas as pl
from jax.experimental.pallas import tpu as pltpu
from jax.sharding import PartitionSpec as P

MESH = pl.DeviceIdType.MESH
F32, BF16 = jnp.float32, jnp.bfloat16
PAIRS = ((0, 0), (1, 1), (0, 1), (0, 2), (1, 3))
PRODUCTS = (0, 1, 4, 5, 8, 2, 3, 9, 6, 7)
PLANES, ROWS, NX = 3, 64, 4096
BLOCKS = 4
PIECES = 2 * PLANES
SEND_AT, MID_AT = 1, 3


def gauss():
    t = np.arange(-16, 17).astype(np.float64)
    e = np.exp(-6.0 * t * t / 256.0)
    return e / e.sum()


G = [float(v) for v in gauss()[16:]]


def x_weights():
    g = gauss()
    w = np.zeros((1280, 128), np.float64)

    def put(row, x, col, coarse):
        t = x - 8 * coarse
        if abs(t) <= 16:
            w[row, col] = g[t + 16]

    for x in range(1024):
        for c in range(128):
            put(x, x, c, c)
    for x in range(128):
        put(1024 + x, x, 126, -2)
        put(1024 + x, x, 127, -1)
        put(1152 + x, 896 + x, 0, 128)
        put(1152 + x, 896 + x, 1, 129)
    w = w.astype(np.float32)
    high = w.astype(jnp.bfloat16)
    low = (w - high.astype(np.float32)).astype(jnp.bfloat16)
    return np.concatenate([high, low], axis=1)


def z_stage(load, row):
    acc = {}

    def add(key, value):
        acc[key] = value if key not in acc else acc[key] + value

    for b in (1, 2, 3):
        near = [load(f, b) for f in range(4)]
        far = [load(f, 8 - b) for f in range(4)]
        for p, (i, j) in enumerate(PAIRS):
            x, y = near[i] * near[j], far[i] * far[j]
            plus, minus = x + y, x - y
            add((p, 0), plus * ((G[b] + G[8 - b]) / 2))
            add((p, 1), minus * ((G[b] - G[8 - b]) / 2))
            add((p, 2), plus * ((G[8 + b] + G[16 - b]) / 2))
            add((p, 3), minus * ((G[8 + b] - G[16 - b]) / 2))
    four = [load(f, 4) for f in range(4)]
    zero = [load(f, 0) for f in range(4)]
    low_half = row < 4
    ends = (row == 0) | (row == 7)
    four_ends = (row < 2) | (row > 5)
    out = []
    for p, (i, j) in enumerate(PAIRS):
        r4, r0 = four[i] * four[j], zero[i] * zero[j]
        r8, r16 = r0 * G[8], r0 * G[16]
        d0, d1 = acc[p, 0] + r4 * G[4], acc[p, 2] + r4 * G[12]
        e0, e1 = acc[p, 1], acc[p, 3]
        s0, down1 = (d0 + e0) + r0 * G[0], (d0 - e0) + r8
        up1, down2 = (d1 + e1) + r8, (d1 - e1) + r16
        u1, u2 = pltpu.roll(up1, 7, 0), pltpu.roll(r16, 6, 0)
        v1, v2 = pltpu.roll(down1, 1, 0), pltpu.roll(down2, 2, 0)
        t1, t2 = jnp.where(low_half, v1, u1), jnp.where(low_half, v2, u2)
        w1, w2 = jnp.where(ends, t1, 0.0), jnp.where(four_ends, t2, 0.0)
        out.append((s0 + ((u1 + v1) - w1) + ((u2 + v2) - w2), t2 + w1))
    return out


def turn(x, shift):
    shift %= 128
    return pltpu.roll(x, shift, 1) if shift else x


def kernel(
    sizes, f_hbm, w_hbm, o_ref, fields, w_ref, held, main_x, leak_x, sent1, got1, sent2, got2, whole, beside,
    f_sem, w_sem, s1_sem, r1_sem, s2_sem, r2_sem, sy_sem, ry_sem,
):
    n_xp, n_zp, n_gy = sizes
    xp, zp, gy = lax.axis_index("xp"), lax.axis_index("zp"), lax.axis_index("gy")
    has_prev, has_next = gy > 0, gy < n_gy - 1

    def tile_copy(unit, h):
        tile = lax.rem(unit, BLOCKS) * 8 + h
        lanes = pl.ds(pl.multiple_of(tile * 128, 128), 128)
        plane = lax.rem(2 * (unit // BLOCKS), 3)
        return pltpu.make_async_copy(
            f_hbm.at[:, plane, :, lanes], fields.at[unit, h], f_sem.at[unit, h]
        )

    def fetch(unit):
        def one(h, carry):
            tile_copy(unit, h).start()
            return carry

        lax.fori_loop(0, 8, one, 0)

    weights = pltpu.make_async_copy(w_hbm, w_ref, w_sem)
    weights.start()
    fetch(0)
    for unit in range(1, BLOCKS):
        fetch(unit)

    barrier = pltpu.get_barrier_semaphore()

    def greet(**where):
        pl.semaphore_signal(barrier, inc=1, device_id=where, device_id_type=MESH)

    for k in range(1, n_zp):
        greet(zp=lax.rem(zp + k, n_zp))
    for k in range(1, n_xp):
        greet(xp=lax.rem(xp + k, n_xp))

    @pl.when(has_prev)
    def _():
        greet(gy=gy - 1)

    @pl.when(has_next)
    def _():
        greet(gy=gy + 1)

    def meet():
        beside_it = has_prev.astype(jnp.int32) + has_next.astype(jnp.int32)
        pl.semaphore_wait(barrier, n_xp + n_zp - 2 + beside_it)

    @pl.when(jnp.logical_not(has_prev))
    def _():
        beside[0] = jnp.zeros(beside.shape[1:], F32)

    @pl.when(jnp.logical_not(has_next))
    def _():
        beside[1] = jnp.zeros(beside.shape[1:], F32)

    row = lax.broadcasted_iota(jnp.int32, (8, 128), 0)
    lane = lax.broadcasted_iota(jnp.int32, (8, 128), 1)
    lane64 = lax.broadcasted_iota(jnp.int32, (64, 128), 1)
    main_x[...] = jnp.zeros(main_x.shape, F32)
    leak_x[...] = jnp.zeros(leak_x.shape, F32)
    got1[PIECES] = jnp.zeros(got1.shape[1:], F32)

    def filter_z(piece, block, h):
        slot = block % 2
        unit = (piece // 2) * BLOCKS + block
        half = lax.rem(piece, 2)
        names = (2 * half, 1 + 2 * half, 2 - half, 3 - 3 * half)

        def load(f, b):
            return fields[unit, h, names[f], pl.ds(b, 8, stride=8), :]

        rows = z_stage(load, row)
        four_ends = (row < 2) | (row > 5)
        groups = [main for main, _ in rows]
        for a in (0, 2):
            groups.append(jnp.where(four_ends, rows[a][1], pltpu.roll(rows[a + 1][1], 4, 0)))
        groups.append(jnp.where(four_ends, rows[4][1], 0.0))
        for k in range(4):
            both = jnp.concatenate(groups[2 * k : 2 * k + 2], axis=0)
            high = both.astype(BF16)
            held[slot, h, 0, k] = high
            held[slot, h, 1, k] = (both - high.astype(F32)).astype(BF16)

    def filter_x(piece, block):
        cells = [held[block % 2, h].reshape(128, 128) for h in range(8)]

        def product(values, weight):
            r = jnp.dot(values, weight, preferred_element_type=F32)
            return r[:64, :128] + r[64:, :128] + r[:64, 128:]

        main_x[block] = product(jnp.concatenate(cells, axis=1), w_ref[0:1024])
        leak_x[block] = product(jnp.concatenate([cells[0], cells[7]], axis=1), w_ref[1024:1280])

    def transpose(piece, block):
        before, after = leak_x[(block + 3) % BLOCKS], leak_x[(block + 1) % BLOCKS]
        x = main_x[block] + jnp.where(lane64 < 2, before, jnp.where(lane64 > 125, after, 0.0))
        y = jnp.transpose(jnp.concatenate([x, pltpu.roll(x, 64, 1)], axis=0))
        sent1[piece, :, block] = y[:64].reshape(8, 8, 128)

    def copy1(piece, to):
        return pltpu.make_async_remote_copy(
            src_ref=sent1.at[piece, to],
            dst_ref=got1.at[piece, zp],
            send_sem=s1_sem.at[piece],
            recv_sem=r1_sem.at[piece],
            device_id={"zp": to},
            device_id_type=MESH,
        )

    def copy2(piece, to):
        return pltpu.make_async_remote_copy(
            src_ref=sent2.at[piece, to],
            dst_ref=got2.at[piece, xp],
            send_sem=s2_sem.at[piece],
            recv_sem=r2_sem.at[piece],
            device_id={"xp": to},
            device_id_type=MESH,
        )

    def all1(piece):
        return pltpu.make_async_remote_copy(
            src_ref=sent1.at[piece, pl.ds(0, n_zp - 1)],
            dst_ref=got1.at[piece, pl.ds(0, n_zp - 1)],
            send_sem=s1_sem.at[piece],
            recv_sem=r1_sem.at[piece],
            device_id={"zp": lax.rem(zp + 1, n_zp)},
            device_id_type=MESH,
        )

    def all2(piece):
        return pltpu.make_async_remote_copy(
            src_ref=sent2.at[piece, pl.ds(0, n_xp - 1)],
            dst_ref=got2.at[piece, pl.ds(0, n_xp - 1)],
            send_sem=s2_sem.at[piece],
            recv_sem=r2_sem.at[piece],
            device_id={"xp": lax.rem(xp + 1, n_xp)},
            device_id_type=MESH,
        )

    def y_copy(side):
        return pltpu.make_async_remote_copy(
            src_ref=whole.at[1 - side],
            dst_ref=beside.at[side],
            send_sem=sy_sem.at[side],
            recv_sem=ry_sem.at[side],
            device_id={"gy": gy + 1 - 2 * side},
            device_id_type=MESH,
        )

    def start(side):
        @pl.when(has_next if side == 0 else has_prev)
        def _():
            y_copy(side).start()

    def send1(piece):
        for k in range(1, n_zp):
            copy1(piece, lax.rem(zp + k, n_zp)).start()
        got1[piece, zp] = sent1[piece, zp]

    def send2(piece):
        for k in range(1, n_xp):
            copy2(piece, lax.rem(xp + k, n_xp)).start()
        got2[piece, xp] = sent2[piece, xp]

    group, within = lane // 8, lax.rem(lane, 8)
    outer = (lane < 2) | (lane > 125) | ((lane > 61) & (lane < 66))
    left = lane < 64
    first_two = lax.rem(lane, 4) < 2

    def middle(piece, block):
        v = [got1[piece, k, block] for k in range(8)]
        for s in (4, 2, 1):
            bit = (group & s) == 0
            for a in range(8):
                if a & s == 0:
                    x, y = v[a], v[a + s]
                    v[a] = jnp.where(bit, x, turn(y, 8 * s))
                    v[a + s] = jnp.where(bit, turn(x, -8 * s), y)
            yield
        out = None
        for j in range(5):
            e, shift = v[5 + j // 2], 8 if j % 2 == 0 else 4
            z = jnp.where(within < 2, turn(e, shift), jnp.where(within > 5, turn(e, -shift), 0.0))
            v[j] = v[j] + jnp.where(outer, 0.0, z)
            z = turn(jnp.where(outer, z, 0.0), 4 * j + 2)
            out = z if out is None else out + z
        yield
        w = [turn(x, 64) for x in v[:5]]
        flip = turn(out, 64)
        rest = (jnp.where(first_two, flip, out), jnp.where(first_two, out, flip))
        for k in range(2):
            low = v if k == 0 else w
            high = w if k == 0 else v
            to = 2 * block + k
            sent2[piece, to, 0] = jnp.where(left, low[0], high[1])
            sent2[piece, to, 1] = jnp.where(left, low[2], high[3])
            sent2[piece, to, 2] = jnp.where(left, low[4], rest[k])

    def last(piece):
        all2(piece).wait_recv()
        plane, half = piece // 2, lax.rem(piece, 2)
        e = [got2[piece, d, 2] for d in range(8)]
        for j in range(5):
            m = [got2[piece, d, j // 2] for d in range(8)]
            near = [turn(x, -2 - 4 * j) for x in e]
            far = [turn(x, 62 - 4 * j) for x in e]
            for g in range(4):
                a, b = m[2 * g], m[2 * g + 1]
                if j % 2 == 0:
                    main = jnp.where(left, a, turn(b, 64))
                else:
                    main = jnp.where(left, turn(a, 64), b)
                z = jnp.where(lane < 2, far[(2 * g + 7) % 8], far[(2 * g + 2) % 8])
                z = jnp.where((lane > 61) & (lane < 64), near[2 * g + 1], z)
                z = jnp.where((lane > 63) & (lane < 66), near[2 * g], z)
                whole[plane, half * 5 + j, :, pl.ds(g * 128, 128)] = main + jnp.where(outer, z, 0.0)

    def run(*parts):
        parts = list(parts)
        while parts:
            parts = [part for part in parts if next(part, parts) is not parts]

    def one_piece(piece, carry):
        before = jnp.where(piece >= SEND_AT, piece - SEND_AT, PIECES)
        early = jnp.where(piece >= MID_AT, piece - MID_AT, PIECES)
        for block in range(BLOCKS):

            @pl.when(lax.rem(piece, 2) == 0)
            def _():
                for h in range(8):
                    tile_copy((piece // 2) * BLOCKS + block, h).wait()

            if block == 0:

                @pl.when(piece == 0)
                def _():
                    weights.wait()

                @pl.when(lax.rem(piece, 2) == 0)
                def _():
                    @pl.when(piece // 2 < PLANES - 1)
                    def _():
                        for later in range(BLOCKS):
                            fetch((piece // 2 + 1) * BLOCKS + later)

            if block == 2:

                @pl.when(piece >= MID_AT)
                def _():
                    all1(early).wait_recv()

            work = []
            if block == 1:
                for part in range(BLOCKS):
                    transpose(before, part)
            if block == 2:
                work = [middle(early, part) for part in range(BLOCKS)]
            filter_x(piece, (block + 3) % BLOCKS)
            for h in range(8):
                work = [part for part in work if next(part, work) is not work]
                filter_z(piece, block, h)
            run(*work)
            if block == 1:

                @pl.when(piece == SEND_AT)
                def _():
                    meet()

                @pl.when(piece >= SEND_AT)
                def _():
                    send1(before)

            if block == 2:

                @pl.when(piece >= MID_AT)
                def _():
                    send2(early)

        return carry

    lax.fori_loop(0, PIECES, one_piece, 0)
    final = PIECES - 1
    filter_x(final, BLOCKS - 1)
    for block in range(BLOCKS):
        transpose(final, block)
    send1(final)

    def rearrange(piece):
        all1(piece).wait_recv()
        run(*[middle(piece, block) for block in range(BLOCKS)])
        send2(piece)

    rearrange(3)
    last(0)
    rearrange(4)
    last(1)
    start(1)
    rearrange(5)
    last(2)
    last(3)
    start(0)
    last(4)
    last(5)

    for side in (0, 1):

        @pl.when(has_prev if side == 0 else has_next)
        def _():
            y_copy(side).wait_recv()

    third = F32(1 / 3)
    scale0 = jnp.where(has_prev, third, F32(1 / 2))
    scale2 = jnp.where(has_next, third, F32(1 / 2))
    for q, p in enumerate(PRODUCTS):
        m0, m2, m1 = whole[0, q], whole[1, q], whole[2, q]
        o_ref[p, 0] = (m0 + m1 + beside[0, q]) * scale0
        o_ref[p, 1] = (m0 + m1 + m2) * third
        o_ref[p, 2] = (m1 + m2 + beside[1, q]) * scale2

    for piece in range(PIECES):
        all1(piece).wait_send()
        all2(piece).wait_send()
    for side in (0, 1):

        @pl.when(has_next if side == 0 else has_prev)
        def _():
            y_copy(side).wait_send()


def solution(mesh):
    placed = P(None, "gy", ("xp", "zp"), None)
    sizes = tuple(mesh.shape[name] for name in ("xp", "zp", "gy"))
    call = pl.pallas_call(
        functools.partial(kernel, sizes),
        out_shape=jax.ShapeDtypeStruct((10, PLANES, 8, 512), F32),
        in_specs=[pl.BlockSpec(memory_space=pl.ANY)] * 2,
        out_specs=pl.BlockSpec(memory_space=pltpu.VMEM),
        scratch_shapes=[
            pltpu.VMEM((PLANES * BLOCKS, 8, 4, ROWS, 128), F32),
            pltpu.VMEM((1280, 256), BF16),
            pltpu.VMEM((2, 8, 2, 4, 16, 128), BF16),
            pltpu.VMEM((BLOCKS, 64, 128), F32),
            pltpu.VMEM((BLOCKS, 64, 128), F32),
            pltpu.VMEM((PIECES + 1, 8, BLOCKS, 8, 128), F32),
            pltpu.VMEM((PIECES + 1, 8, BLOCKS, 8, 128), F32),
            pltpu.VMEM((PIECES + 1, 8, 3, 8, 128), F32),
            pltpu.VMEM((PIECES, 8, 3, 8, 128), F32),
            pltpu.VMEM((PLANES, 10, 8, 512), F32),
            pltpu.VMEM((2, 10, 8, 512), F32),
            pltpu.SemaphoreType.DMA((PLANES * BLOCKS, 8)),
            pltpu.SemaphoreType.DMA,
            pltpu.SemaphoreType.DMA((PIECES,)),
            pltpu.SemaphoreType.DMA((PIECES,)),
            pltpu.SemaphoreType.DMA((PIECES,)),
            pltpu.SemaphoreType.DMA((PIECES,)),
            pltpu.SemaphoreType.DMA((2,)),
            pltpu.SemaphoreType.DMA((2,)),
        ],
        compiler_params=pltpu.CompilerParams(
            collective_id=0, has_side_effects=True, vmem_limit_bytes=60 * 2**20
        ),
    )
    weights = x_weights()

    def per_device(fields):
        return call(fields, jnp.asarray(weights))

    return jax.shard_map(
        per_device, mesh=mesh, in_specs=(placed,), out_specs=placed, check_vma=False
    )
```

```python
import functools

import jax
import jax.numpy as jnp
import numpy as np
from jax import lax
from jax.experimental import pallas as pl
from jax.experimental.pallas import tpu as pltpu
from jax.sharding import PartitionSpec as P

MESH = pl.DeviceIdType.MESH
F32, BF16 = jnp.float32, jnp.bfloat16
PAIRS = ((0, 0), (1, 1), (0, 1), (0, 2), (1, 3))
PRODUCTS = (0, 1, 4, 5, 8, 2, 3, 9, 6, 7)
PLANES, ROWS, NX = 3, 64, 4096
BLOCKS = 4
PIECES = 2 * PLANES
STEPS = PIECES * BLOCKS
SEND_AT, MID_AT, LAST_AT = 4, 14, 27


def gauss():
    t = np.arange(-16, 17).astype(np.float64)
    e = np.exp(-6.0 * t * t / 256.0)
    return e / e.sum()


G = [float(v) for v in gauss()[16:]]


def x_weights():
    g = gauss()
    w = np.zeros((1280, 128), np.float64)

    def put(row, x, col, coarse):
        t = x - 8 * coarse
        if abs(t) <= 16:
            w[row, col] = g[t + 16]

    for x in range(1024):
        for c in range(128):
            put(x, x, c, c)
    for x in range(128):
        put(1024 + x, x, 126, -2)
        put(1024 + x, x, 127, -1)
        put(1152 + x, 896 + x, 0, 128)
        put(1152 + x, 896 + x, 1, 129)
    w = w.astype(np.float32)
    high = w.astype(jnp.bfloat16)
    low = (w - high.astype(np.float32)).astype(jnp.bfloat16)
    return np.concatenate([high, low], axis=1)


def z_stage(load, row):
    acc = {}

    def add(key, value):
        acc[key] = value if key not in acc else acc[key] + value

    for b in (1, 2, 3):
        near = [load(f, b) for f in range(4)]
        far = [load(f, 8 - b) for f in range(4)]
        for p, (i, j) in enumerate(PAIRS):
            x, y = near[i] * near[j], far[i] * far[j]
            plus, minus = x + y, x - y
            add((p, 0), plus * ((G[b] + G[8 - b]) / 2))
            add((p, 1), minus * ((G[b] - G[8 - b]) / 2))
            add((p, 2), plus * ((G[8 + b] + G[16 - b]) / 2))
            add((p, 3), minus * ((G[8 + b] - G[16 - b]) / 2))
    four = [load(f, 4) for f in range(4)]
    zero = [load(f, 0) for f in range(4)]
    low_half = row < 4
    ends = (row == 0) | (row == 7)
    four_ends = (row < 2) | (row > 5)
    out = []
    for p, (i, j) in enumerate(PAIRS):
        r4, r0 = four[i] * four[j], zero[i] * zero[j]
        r8, r16 = r0 * G[8], r0 * G[16]
        d0, d1 = acc[p, 0] + r4 * G[4], acc[p, 2] + r4 * G[12]
        e0, e1 = acc[p, 1], acc[p, 3]
        s0, down1 = (d0 + e0) + r0 * G[0], (d0 - e0) + r8
        up1, down2 = (d1 + e1) + r8, (d1 - e1) + r16
        u1, u2 = pltpu.roll(up1, 7, 0), pltpu.roll(r16, 6, 0)
        v1, v2 = pltpu.roll(down1, 1, 0), pltpu.roll(down2, 2, 0)
        t1, t2 = jnp.where(low_half, v1, u1), jnp.where(low_half, v2, u2)
        w1, w2 = jnp.where(ends, t1, 0.0), jnp.where(four_ends, t2, 0.0)
        out.append((s0 + ((u1 + v1) - w1) + ((u2 + v2) - w2), t2 + w1))
    return out


def far_first(n):
    return sorted(range(1, n), key=lambda k: -min(k, n - k))


def turn(x, shift):
    shift %= 128
    return pltpu.roll(x, shift, 1) if shift else x


def kernel(
    sizes, f_hbm, w_hbm, o_ref, fields, w_ref, held, main_x, leak_x, sent1, got1, sent2, got2, whole, beside,
    f_sem, w_sem, s1_sem, r1_sem, s2_sem, r2_sem, sy_sem, ry_sem,
):
    n_xp, n_zp, n_gy = sizes
    xp, zp, gy = lax.axis_index("xp"), lax.axis_index("zp"), lax.axis_index("gy")
    has_prev, has_next = gy > 0, gy < n_gy - 1

    def fetch(unit):
        x_tiles = pl.ds(pl.multiple_of(lax.rem(unit, BLOCKS) * 8, 8), 8)
        plane = lax.rem(2 * (unit // BLOCKS), 3)
        return pltpu.make_async_copy(
            f_hbm.at[:, plane, :, x_tiles],
            fields.at[unit].reshape(4, 8, 9, 8, 128).at[:, :, pl.ds(0, 8)],
            f_sem.at[unit],
        )

    weights = pltpu.make_async_copy(w_hbm, w_ref, w_sem)
    weights.start()
    for unit in range(BLOCKS):
        fetch(unit).start()

    barrier = pltpu.get_barrier_semaphore()

    def greet(**where):
        pl.semaphore_signal(barrier, inc=1, device_id=where, device_id_type=MESH)

    for k in range(1, n_zp):
        greet(zp=lax.rem(zp + k, n_zp))
    for k in range(1, n_xp):
        greet(xp=lax.rem(xp + k, n_xp))

    @pl.when(has_prev)
    def _():
        greet(gy=gy - 1)

    @pl.when(has_next)
    def _():
        greet(gy=gy + 1)

    def meet():
        beside_it = has_prev.astype(jnp.int32) + has_next.astype(jnp.int32)
        pl.semaphore_wait(barrier, n_xp + n_zp - 2 + beside_it)

    @pl.when(jnp.logical_not(has_prev))
    def _():
        beside[0] = jnp.zeros(beside.shape[1:], F32)

    @pl.when(jnp.logical_not(has_next))
    def _():
        beside[1] = jnp.zeros(beside.shape[1:], F32)

    row = lax.broadcasted_iota(jnp.int32, (8, 128), 0)
    lane = lax.broadcasted_iota(jnp.int32, (8, 128), 1)
    lane64 = lax.broadcasted_iota(jnp.int32, (64, 128), 1)
    def filter_z(step, h):
        piece, block = step // BLOCKS, lax.rem(step, BLOCKS)
        slot = lax.rem(step, 2)
        unit = (piece // 2) * BLOCKS + block
        half = lax.rem(piece, 2)
        names = (2 * half, 1 + 2 * half, 2 - half, 3 - 3 * half)

        def load(f, b):
            return fields[unit, pl.ds(names[f] * 576 + h * 8 + b, 8, stride=72), :]

        rows = z_stage(load, row)
        four_ends = (row < 2) | (row > 5)
        groups = [main for main, _ in rows]
        for a in (0, 2):
            groups.append(jnp.where(four_ends, rows[a][1], pltpu.roll(rows[a + 1][1], 4, 0)))
        groups.append(jnp.where(four_ends, rows[4][1], 0.0))
        for k in range(4):
            both = jnp.concatenate(groups[2 * k : 2 * k + 2], axis=0)
            high = both.astype(BF16)
            held[slot, h, 0, k] = high
            held[slot, h, 1, k] = (both - high.astype(F32)).astype(BF16)

    def filter_x(step):
        block, slot = lax.rem(step, BLOCKS), lax.rem(step, 2)
        cells = [held[slot, h].reshape(128, 128) for h in range(8)]

        def product(values, weight):
            r = jnp.dot(values, weight, preferred_element_type=F32)
            return r[:64, :128] + r[64:, :128] + r[:64, 128:]

        main_x[block] = product(jnp.concatenate(cells, axis=1), w_ref[0:1024])
        leak_x[block] = product(jnp.concatenate([cells[0], cells[7]], axis=1), w_ref[1024:1280])

    def transpose(piece, pair):
        both = []
        for block in (2 * pair, 2 * pair + 1):
            before, after = leak_x[(block + 3) % BLOCKS], leak_x[(block + 1) % BLOCKS]
            both.append(main_x[block] + jnp.where(lane64 < 2, before, jnp.where(lane64 > 125, after, 0.0)))
        y = jnp.transpose(jnp.concatenate(both, axis=0))
        for k in range(2):
            sent1[piece, :, 2 * pair + k] = y[64 * k : 64 * k + 64].reshape(8, 8, 128)

    def copy1(piece, to):
        return pltpu.make_async_remote_copy(
            src_ref=sent1.at[piece, to],
            dst_ref=got1.at[piece, zp],
            send_sem=s1_sem.at[piece],
            recv_sem=r1_sem.at[piece],
            device_id={"zp": to},
            device_id_type=MESH,
        )

    def copy2(piece, to):
        return pltpu.make_async_remote_copy(
            src_ref=sent2.at[piece, to],
            dst_ref=got2.at[piece, xp],
            send_sem=s2_sem.at[piece],
            recv_sem=r2_sem.at[piece],
            device_id={"xp": to},
            device_id_type=MESH,
        )

    def all1(piece):
        return pltpu.make_async_remote_copy(
            src_ref=sent1.at[piece, pl.ds(0, n_zp - 1)],
            dst_ref=got1.at[piece, pl.ds(0, n_zp - 1)],
            send_sem=s1_sem.at[piece],
            recv_sem=r1_sem.at[piece],
            device_id={"zp": lax.rem(zp + 1, n_zp)},
            device_id_type=MESH,
        )

    def all2(piece):
        return pltpu.make_async_remote_copy(
            src_ref=sent2.at[piece, pl.ds(0, n_xp - 1)],
            dst_ref=got2.at[piece, pl.ds(0, n_xp - 1)],
            send_sem=s2_sem.at[piece],
            recv_sem=r2_sem.at[piece],
            device_id={"xp": lax.rem(xp + 1, n_xp)},
            device_id_type=MESH,
        )

    def y_copy(side):
        return pltpu.make_async_remote_copy(
            src_ref=whole.at[1 - side],
            dst_ref=beside.at[side],
            send_sem=sy_sem.at[side],
            recv_sem=ry_sem.at[side],
            device_id={"gy": gy + 1 - 2 * side},
            device_id_type=MESH,
        )

    def start(side):
        @pl.when(has_next if side == 0 else has_prev)
        def _():
            y_copy(side).start()

    def send1(piece):
        for k in far_first(n_zp):
            copy1(piece, lax.rem(zp + k, n_zp)).start()
        got1[piece, zp] = sent1[piece, zp]

    def send2(piece):
        for k in far_first(n_xp):
            copy2(piece, lax.rem(xp + k, n_xp)).start()
        got2[piece, xp] = sent2[piece, xp]

    group, within = lane // 8, lax.rem(lane, 8)
    outer = (lane < 2) | (lane > 125) | ((lane > 61) & (lane < 66))
    left = lane < 64
    first_two = lax.rem(lane, 4) < 2

    def middle(piece, block):
        v = [got1[piece, k, block] for k in range(8)]
        for s in (4, 2, 1):
            bit = (group & s) == 0
            for a in range(8):
                if a & s == 0:
                    x, y = v[a], v[a + s]
                    v[a] = jnp.where(bit, x, turn(y, 8 * s))
                    v[a + s] = jnp.where(bit, turn(x, -8 * s), y)
            yield
        out = None
        for j in range(5):
            e, shift = v[5 + j // 2], 8 if j % 2 == 0 else 4
            z = jnp.where(within < 2, turn(e, shift), jnp.where(within > 5, turn(e, -shift), 0.0))
            v[j] = v[j] + jnp.where(outer, 0.0, z)
            z = turn(jnp.where(outer, z, 0.0), 4 * j + 2)
            out = z if out is None else out + z
        yield
        to = 4 * (block // 2) + block % 2
        for k in range(3):
            x, y = v[2 * k], v[2 * k + 1] if k < 2 else out
            swap = turn(jnp.where(left, y, x), 64)
            if k < 2:
                low, high = swap, y
            else:
                low, high = jnp.where(first_two, swap, y), jnp.where(first_two, y, swap)
            sent2[piece, to, k] = jnp.where(left, x, low)
            sent2[piece, to + 2, k] = jnp.where(left, swap, high)

    def last(piece):
        all2(piece).wait_recv()
        plane, half = piece // 2, lax.rem(piece, 2)
        e = [got2[piece, d, 2] for d in range(8)]
        around = []
        for g in range(4):
            near = jnp.where(first_two, e[2 * g + 1], e[2 * g])
            far = jnp.where(first_two, e[(2 * g + 2) % 8], e[(2 * g + 7) % 8])
            around.append(jnp.where(left, turn(far, 64), near))
        for j in range(5):
            for g in range(4):
                a, b = got2[piece, 2 * g, j // 2], got2[piece, 2 * g + 1, j // 2]
                main = jnp.where(left, a, turn(b, 64)) if j % 2 == 0 else jnp.where(left, turn(a, 64), b)
                z = turn(around[g], -2 - 4 * j)
                whole[plane, half * 5 + j, :, pl.ds(g * 128, 128)] = main + jnp.where(outer, z, 0.0)

    third = F32(1 / 3)
    scale0 = jnp.where(has_prev, third, F32(1 / 2))
    scale2 = jnp.where(has_next, third, F32(1 / 2))

    def box(half):
        for q in range(5 * half, 5 * half + 5):
            p, m0, m2, m1 = PRODUCTS[q], whole[0, q], whole[1, q], whole[2, q]
            o_ref[p, 0] = (m0 + m1 + beside[0, q]) * scale0
            o_ref[p, 1] = (m0 + m1 + m2) * third
            o_ref[p, 2] = (m1 + m2 + beside[1, q]) * scale2

    def one_step(step, carry):
        block = lax.rem(step, BLOCKS)

        @pl.when((step < STEPS) & (lax.rem(step, 2 * BLOCKS) < BLOCKS))
        def _():
            fetch((step // (2 * BLOCKS)) * BLOCKS + block).wait()

        @pl.when(step == 0)
        def _():
            weights.wait()

        @pl.when(step < STEPS)
        def _():
            filter_x(step + STEPS - 1)
            for h in range(8):
                filter_z(step, h)

        @pl.when(step == STEPS)
        def _():
            filter_x(step - 1)

        @pl.when(step == SEND_AT)
        def _():
            meet()

        @pl.when((block == SEND_AT % BLOCKS) & (step >= SEND_AT) & (step <= STEPS))
        def _():
            piece = (step - SEND_AT) // BLOCKS
            transpose(piece, 0)
            transpose(piece, 1)
            send1(piece)

        @pl.when((step >= 1) & (step <= (PLANES - 1) * BLOCKS))
        def _():
            fetch(step + BLOCKS - 1).start()

        @pl.when((block == MID_AT % BLOCKS) & (step >= MID_AT) & (step < MID_AT + PIECES * BLOCKS))
        def _():
            piece = (step - MID_AT) // BLOCKS
            all1(piece).wait_recv()
            work = [middle(piece, part) for part in range(BLOCKS)]
            while work:
                work = [part for part in work if next(part, work) is not work]
            send2(piece)

        @pl.when((step == LAST_AT) | (step == LAST_AT + BLOCKS) | (step >= LAST_AT + 2 * BLOCKS))
        def _():
            last(jnp.where(step > LAST_AT + BLOCKS, step - LAST_AT - 2 * BLOCKS + 2, (step - LAST_AT) // BLOCKS))

        @pl.when(step == LAST_AT + BLOCKS)
        def _():
            start(1)

        @pl.when(step == LAST_AT + 2 * BLOCKS + 1)
        def _():
            start(0)

        return carry

    lax.fori_loop(0, LAST_AT + 2 * BLOCKS + 3, one_step, 0)
    for side in (0, 1):

        @pl.when(has_prev if side == 0 else has_next)
        def _():
            y_copy(side).wait_recv()

    box(0)
    last(PIECES - 1)
    box(1)

    for piece in range(PIECES):
        all1(piece).wait_send()
        all2(piece).wait_send()
    for side in (0, 1):

        @pl.when(has_next if side == 0 else has_prev)
        def _():
            y_copy(side).wait_send()


def solution(mesh):
    placed = P(None, "gy", ("xp", "zp"), None)
    sizes = tuple(mesh.shape[name] for name in ("xp", "zp", "gy"))
    call = pl.pallas_call(
        functools.partial(kernel, sizes),
        out_shape=pltpu.VMEM((10, PLANES, 8, 512), F32),
        in_specs=[pl.BlockSpec(memory_space=pl.ANY)] * 2,
        out_specs=pl.BlockSpec(memory_space=pltpu.VMEM),
        scratch_shapes=[
            pltpu.VMEM((PLANES * BLOCKS, 4 * ROWS * 9, 128), F32),
            pltpu.VMEM((1280, 256), BF16),
            pltpu.VMEM((2, 8, 2, 4, 16, 128), BF16),
            pltpu.VMEM((BLOCKS, 64, 128), F32),
            pltpu.VMEM((BLOCKS, 64, 128), F32),
            pltpu.VMEM((PIECES, 8, BLOCKS, 8, 128), F32),
            pltpu.VMEM((PIECES, 8, BLOCKS, 8, 128), F32),
            pltpu.VMEM((PIECES, 8, 3, 8, 128), F32),
            pltpu.VMEM((PIECES, 8, 3, 8, 128), F32),
            pltpu.VMEM((PLANES, 10, 8, 512), F32),
            pltpu.VMEM((2, 10, 8, 512), F32),
            pltpu.SemaphoreType.DMA((PLANES * BLOCKS,)),
            pltpu.SemaphoreType.DMA,
            pltpu.SemaphoreType.DMA((PIECES,)),
            pltpu.SemaphoreType.DMA((PIECES,)),
            pltpu.SemaphoreType.DMA((PIECES,)),
            pltpu.SemaphoreType.DMA((PIECES,)),
            pltpu.SemaphoreType.DMA((2,)),
            pltpu.SemaphoreType.DMA((2,)),
        ],
        compiler_params=pltpu.CompilerParams(
            collective_id=0, has_side_effects=True, vmem_limit_bytes=60 * 2**20
        ),
    )
    weights = x_weights()

    def per_device(fields):
        tiles = fields.reshape(4, PLANES, ROWS // 8, 8, NX // 128, 128).transpose(0, 1, 2, 4, 3, 5)
        return call(tiles, jnp.asarray(weights))

    return jax.shard_map(
        per_device, mesh=mesh, in_specs=(placed,), out_specs=placed, check_vma=False
    )
```

```python
import functools

import jax
import jax.numpy as jnp
import numpy as np
from jax import lax
from jax.experimental import pallas as pl
from jax.experimental.pallas import tpu as pltpu
from jax.sharding import PartitionSpec as P

MESH = pl.DeviceIdType.MESH
F32, BF16 = jnp.float32, jnp.bfloat16
PAIRS = ((0, 0), (1, 1), (0, 1), (0, 2), (1, 3))
PRODUCTS = (0, 1, 4, 5, 8, 2, 3, 9, 6, 7)
PLANES, ROWS, NX = 3, 64, 4096
BLOCKS = 4
PIECES = 2 * PLANES
STEPS = PIECES * BLOCKS
SEND_AT, MID_AT, LAST_AT = 4, 14, 27


def gauss():
    t = np.arange(-16, 17).astype(np.float64)
    e = np.exp(-6.0 * t * t / 256.0)
    return e / e.sum()


G = [float(v) for v in gauss()[16:]]


def x_weights():
    g = gauss()
    w = np.zeros((1280, 128), np.float64)

    def put(row, x, col, coarse):
        t = x - 8 * coarse
        if abs(t) <= 16:
            w[row, col] = g[t + 16]

    for x in range(1024):
        for c in range(128):
            put(x, x, c, c)
    for x in range(128):
        put(1024 + x, x, 126, -2)
        put(1024 + x, x, 127, -1)
        put(1152 + x, 896 + x, 0, 128)
        put(1152 + x, 896 + x, 1, 129)
    w = w.astype(np.float32)
    high = w.astype(jnp.bfloat16)
    low = (w - high.astype(np.float32)).astype(jnp.bfloat16)
    return np.concatenate([high, low], axis=1)


def z_stage(load, row):
    acc = {}

    def add(key, value):
        acc[key] = value if key not in acc else acc[key] + value

    for b in (1, 2, 3):
        near = [load(f, b) for f in range(4)]
        far = [load(f, 8 - b) for f in range(4)]
        for p, (i, j) in enumerate(PAIRS):
            x, y = near[i] * near[j], far[i] * far[j]
            plus, minus = x + y, x - y
            add((p, 0), plus * ((G[b] + G[8 - b]) / 2))
            add((p, 1), minus * ((G[b] - G[8 - b]) / 2))
            add((p, 2), plus * ((G[8 + b] + G[16 - b]) / 2))
            add((p, 3), minus * ((G[8 + b] - G[16 - b]) / 2))
    four = [load(f, 4) for f in range(4)]
    zero = [load(f, 0) for f in range(4)]
    low_half = row < 4
    ends = (row == 0) | (row == 7)
    four_ends = (row < 2) | (row > 5)
    out = []
    for p, (i, j) in enumerate(PAIRS):
        r4, r0 = four[i] * four[j], zero[i] * zero[j]
        r8, r16 = r0 * G[8], r0 * G[16]
        d0, d1 = acc[p, 0] + r4 * G[4], acc[p, 2] + r4 * G[12]
        e0, e1 = acc[p, 1], acc[p, 3]
        s0, down1 = (d0 + e0) + r0 * G[0], (d0 - e0) + r8
        up1, down2 = (d1 + e1) + r8, (d1 - e1) + r16
        u1, u2 = pltpu.roll(up1, 7, 0), pltpu.roll(r16, 6, 0)
        v1, v2 = pltpu.roll(down1, 1, 0), pltpu.roll(down2, 2, 0)
        t1, t2 = jnp.where(low_half, v1, u1), jnp.where(low_half, v2, u2)
        w1, w2 = jnp.where(ends, t1, 0.0), jnp.where(four_ends, t2, 0.0)
        out.append((s0 + ((u1 + v1) - w1) + ((u2 + v2) - w2), t2 + w1))
    return out


def far_first(n):
    return sorted(range(1, n), key=lambda k: -min(k, n - k))


def turn(x, shift):
    shift %= 128
    return pltpu.roll(x, shift, 1) if shift else x


def kernel(
    sizes, f_hbm, w_hbm, o_ref, fields, w_ref, held, main_x, leak_x, sent1, got1, sent2, got2, whole, beside,
    f_sem, w_sem, s1_sem, r1_sem, s2_sem, r2_sem, sy_sem, ry_sem,
):
    n_xp, n_zp, n_gy = sizes
    xp, zp, gy = lax.axis_index("xp"), lax.axis_index("zp"), lax.axis_index("gy")
    has_prev, has_next = gy > 0, gy < n_gy - 1

    def fetch(unit):
        x_tiles = pl.ds(pl.multiple_of(lax.rem(unit, BLOCKS) * 8, 8), 8)
        plane = lax.rem(2 * (unit // BLOCKS), 3)
        return pltpu.make_async_copy(
            f_hbm.at[:, plane, :, x_tiles],
            fields.at[unit].reshape(4, 8, 9, 8, 128).at[:, :, pl.ds(0, 8)],
            f_sem.at[unit],
        )

    weights = pltpu.make_async_copy(w_hbm, w_ref, w_sem)
    weights.start()
    for unit in range(PLANES * BLOCKS):
        fetch(unit).start()

    barrier = pltpu.get_barrier_semaphore()

    def greet(**where):
        pl.semaphore_signal(barrier, inc=1, device_id=where, device_id_type=MESH)

    for k in range(1, n_zp):
        greet(zp=lax.rem(zp + k, n_zp))
    for k in range(1, n_xp):
        greet(xp=lax.rem(xp + k, n_xp))

    @pl.when(has_prev)
    def _():
        greet(gy=gy - 1)

    @pl.when(has_next)
    def _():
        greet(gy=gy + 1)

    def meet():
        beside_it = has_prev.astype(jnp.int32) + has_next.astype(jnp.int32)
        pl.semaphore_wait(barrier, n_xp + n_zp - 2 + beside_it)

    @pl.when(jnp.logical_not(has_prev))
    def _():
        beside[0] = jnp.zeros(beside.shape[1:], F32)

    @pl.when(jnp.logical_not(has_next))
    def _():
        beside[1] = jnp.zeros(beside.shape[1:], F32)

    row = lax.broadcasted_iota(jnp.int32, (8, 128), 0)
    lane = lax.broadcasted_iota(jnp.int32, (8, 128), 1)
    lane64 = lax.broadcasted_iota(jnp.int32, (64, 128), 1)
    def filter_z(step, h):
        piece, block = step // BLOCKS, lax.rem(step, BLOCKS)
        slot = lax.rem(step, 2)
        unit = (piece // 2) * BLOCKS + block
        half = lax.rem(piece, 2)
        names = (2 * half, 1 + 2 * half, 2 - half, 3 - 3 * half)

        def load(f, b):
            return fields[unit, pl.ds(names[f] * 576 + h * 8 + b, 8, stride=72), :]

        rows = z_stage(load, row)
        four_ends = (row < 2) | (row > 5)
        groups = [main for main, _ in rows]
        for a in (0, 2):
            groups.append(jnp.where(four_ends, rows[a][1], pltpu.roll(rows[a + 1][1], 4, 0)))
        groups.append(jnp.where(four_ends, rows[4][1], 0.0))
        for k in range(4):
            both = jnp.concatenate(groups[2 * k : 2 * k + 2], axis=0)
            high = both.astype(BF16)
            held[slot, h, 0, k] = high
            held[slot, h, 1, k] = (both - high.astype(F32)).astype(BF16)

    def filter_x(step):
        block, slot = lax.rem(step, BLOCKS), lax.rem(step, 2)
        cells = [held[slot, h].reshape(128, 128) for h in range(8)]

        def product(values, weight):
            r = jnp.dot(values, weight, preferred_element_type=F32)
            return r[:64, :128] + r[64:, :128] + r[:64, 128:]

        main_x[block] = product(jnp.concatenate(cells, axis=1), w_ref[0:1024])
        leak_x[block] = product(jnp.concatenate([cells[0], cells[7]], axis=1), w_ref[1024:1280])

    def transpose(piece, pair):
        both = []
        for block in (2 * pair, 2 * pair + 1):
            before, after = leak_x[(block + 3) % BLOCKS], leak_x[(block + 1) % BLOCKS]
            both.append(main_x[block] + jnp.where(lane64 < 2, before, jnp.where(lane64 > 125, after, 0.0)))
        y = jnp.transpose(jnp.concatenate(both, axis=0))
        for k in range(2):
            sent1[piece, :, 2 * pair + k] = y[64 * k : 64 * k + 64].reshape(8, 8, 128)

    def copy1(piece, to):
        return pltpu.make_async_remote_copy(
            src_ref=sent1.at[piece, to],
            dst_ref=got1.at[piece, zp],
            send_sem=s1_sem.at[piece],
            recv_sem=r1_sem.at[piece],
            device_id={"zp": to},
            device_id_type=MESH,
        )

    def copy2(piece, to):
        return pltpu.make_async_remote_copy(
            src_ref=sent2.at[piece, to],
            dst_ref=got2.at[piece, xp],
            send_sem=s2_sem.at[piece],
            recv_sem=r2_sem.at[piece],
            device_id={"xp": to},
            device_id_type=MESH,
        )

    def all1(piece):
        return pltpu.make_async_remote_copy(
            src_ref=sent1.at[piece, pl.ds(0, n_zp - 1)],
            dst_ref=got1.at[piece, pl.ds(0, n_zp - 1)],
            send_sem=s1_sem.at[piece],
            recv_sem=r1_sem.at[piece],
            device_id={"zp": lax.rem(zp + 1, n_zp)},
            device_id_type=MESH,
        )

    def all2(piece):
        return pltpu.make_async_remote_copy(
            src_ref=sent2.at[piece, pl.ds(0, n_xp - 1)],
            dst_ref=got2.at[piece, pl.ds(0, n_xp - 1)],
            send_sem=s2_sem.at[piece],
            recv_sem=r2_sem.at[piece],
            device_id={"xp": lax.rem(xp + 1, n_xp)},
            device_id_type=MESH,
        )

    def y_copy(side):
        return pltpu.make_async_remote_copy(
            src_ref=whole.at[1 - side],
            dst_ref=beside.at[side],
            send_sem=sy_sem.at[side],
            recv_sem=ry_sem.at[side],
            device_id={"gy": gy + 1 - 2 * side},
            device_id_type=MESH,
        )

    def start(side):
        @pl.when(has_next if side == 0 else has_prev)
        def _():
            y_copy(side).start()

    def send1(piece):
        for k in far_first(n_zp):
            copy1(piece, lax.rem(zp + k, n_zp)).start()
        got1[piece, zp] = sent1[piece, zp]

    def send2(piece):
        for k in far_first(n_xp):
            copy2(piece, lax.rem(xp + k, n_xp)).start()
        got2[piece, xp] = sent2[piece, xp]

    group, within = lane // 8, lax.rem(lane, 8)
    outer = (lane < 2) | (lane > 125) | ((lane > 61) & (lane < 66))
    left = lane < 64
    first_two = lax.rem(lane, 4) < 2

    def middle(piece, block):
        v = [turn(got1[piece, k, block], 8 * k) for k in range(8)]
        yield
        for s in (1, 2, 4):
            bit = (group & s) == 0
            v = [jnp.where(bit, v[k], v[(k + s) % 8]) for k in range(8)]
        yield
        v = [v[-j % 8] for j in range(8)]
        out = None
        for j in range(5):
            e, back, shift = v[5 + j // 2], -8 * (5 + j // 2), 8 if j % 2 == 0 else 4
            up, down = turn(e, back + shift), turn(e, back - shift)
            z = jnp.where(within < 2, up, jnp.where(within > 5, down, 0.0))
            v[j] = turn(v[j], -8 * j) + jnp.where(outer, 0.0, z)
            z = turn(jnp.where(outer, z, 0.0), 4 * j + 2)
            out = z if out is None else out + z
        yield
        to = 4 * (block // 2) + block % 2
        for k in range(3):
            x, y = v[2 * k], v[2 * k + 1] if k < 2 else out
            swap = turn(jnp.where(left, y, x), 64)
            if k < 2:
                low, high = swap, y
            else:
                low, high = jnp.where(first_two, swap, y), jnp.where(first_two, y, swap)
            sent2[piece, to, k] = jnp.where(left, x, low)
            sent2[piece, to + 2, k] = jnp.where(left, swap, high)

    def last(piece):
        all2(piece).wait_recv()
        plane, half = piece // 2, lax.rem(piece, 2)
        e = [got2[piece, d, 2] for d in range(8)]
        around = []
        for g in range(4):
            near = jnp.where(first_two, e[2 * g + 1], e[2 * g])
            far = jnp.where(first_two, e[(2 * g + 2) % 8], e[(2 * g + 7) % 8])
            around.append(jnp.where(left, turn(far, 64), near))
        for j in range(5):
            for g in range(4):
                a, b = got2[piece, 2 * g, j // 2], got2[piece, 2 * g + 1, j // 2]
                main = jnp.where(left, a, turn(b, 64)) if j % 2 == 0 else jnp.where(left, turn(a, 64), b)
                z = turn(around[g], -2 - 4 * j)
                whole[plane, half * 5 + j, :, pl.ds(g * 128, 128)] = main + jnp.where(outer, z, 0.0)

    third = F32(1 / 3)
    scale0 = jnp.where(has_prev, third, F32(1 / 2))
    scale2 = jnp.where(has_next, third, F32(1 / 2))

    def box(half):
        for q in range(5 * half, 5 * half + 5):
            p, m0, m2, m1 = PRODUCTS[q], whole[0, q], whole[1, q], whole[2, q]
            o_ref[p, 0] = (m0 + m1 + beside[0, q]) * scale0
            o_ref[p, 1] = (m0 + m1 + m2) * third
            o_ref[p, 2] = (m1 + m2 + beside[1, q]) * scale2

    def one_step(step, carry):
        block = lax.rem(step, BLOCKS)

        @pl.when((step < STEPS) & (lax.rem(step, 2 * BLOCKS) < BLOCKS))
        def _():
            fetch((step // (2 * BLOCKS)) * BLOCKS + block).wait()

        @pl.when(step == 0)
        def _():
            weights.wait()

        @pl.when(step < STEPS)
        def _():
            filter_x(step + STEPS - 1)
            for h in range(8):
                filter_z(step, h)

        @pl.when(step == STEPS)
        def _():
            filter_x(step - 1)

        @pl.when(step == SEND_AT)
        def _():
            meet()

        @pl.when((block == SEND_AT % BLOCKS) & (step >= SEND_AT) & (step <= STEPS))
        def _():
            piece = (step - SEND_AT) // BLOCKS
            transpose(piece, 0)
            transpose(piece, 1)
            send1(piece)

        @pl.when((block == MID_AT % BLOCKS) & (step >= MID_AT) & (step < MID_AT + PIECES * BLOCKS))
        def _():
            piece = (step - MID_AT) // BLOCKS
            all1(piece).wait_recv()
            work = [middle(piece, part) for part in range(BLOCKS)]
            while work:
                work = [part for part in work if next(part, work) is not work]
            send2(piece)

        @pl.when((step == LAST_AT) | (step == LAST_AT + BLOCKS) | (step >= LAST_AT + 2 * BLOCKS))
        def _():
            last(jnp.where(step > LAST_AT + BLOCKS, step - LAST_AT - 2 * BLOCKS + 2, (step - LAST_AT) // BLOCKS))

        @pl.when(step == LAST_AT + BLOCKS)
        def _():
            start(1)

        @pl.when(step == LAST_AT + 2 * BLOCKS + 1)
        def _():
            start(0)

        return carry

    lax.fori_loop(0, LAST_AT + 2 * BLOCKS + 3, one_step, 0)
    for side in (0, 1):

        @pl.when(has_prev if side == 0 else has_next)
        def _():
            y_copy(side).wait_recv()

    box(0)
    last(PIECES - 1)
    box(1)

    for piece in range(PIECES):
        all1(piece).wait_send()
        all2(piece).wait_send()
    for side in (0, 1):

        @pl.when(has_next if side == 0 else has_prev)
        def _():
            y_copy(side).wait_send()


def solution(mesh):
    placed = P(None, "gy", ("xp", "zp"), None)
    sizes = tuple(mesh.shape[name] for name in ("xp", "zp", "gy"))
    call = pl.pallas_call(
        functools.partial(kernel, sizes),
        out_shape=pltpu.VMEM((10, PLANES, 8, 512), F32),
        in_specs=[pl.BlockSpec(memory_space=pl.ANY)] * 2,
        out_specs=pl.BlockSpec(memory_space=pltpu.VMEM),
        scratch_shapes=[
            pltpu.VMEM((PLANES * BLOCKS, 4 * ROWS * 9, 128), F32),
            pltpu.VMEM((1280, 256), BF16),
            pltpu.VMEM((2, 8, 2, 4, 16, 128), BF16),
            pltpu.VMEM((BLOCKS, 64, 128), F32),
            pltpu.VMEM((BLOCKS, 64, 128), F32),
            pltpu.VMEM((PIECES, 8, BLOCKS, 8, 128), F32),
            pltpu.VMEM((PIECES, 8, BLOCKS, 8, 128), F32),
            pltpu.VMEM((PIECES, 8, 3, 8, 128), F32),
            pltpu.VMEM((PIECES, 8, 3, 8, 128), F32),
            pltpu.VMEM((PLANES, 10, 8, 512), F32),
            pltpu.VMEM((2, 10, 8, 512), F32),
            pltpu.SemaphoreType.DMA((PLANES * BLOCKS,)),
            pltpu.SemaphoreType.DMA,
            pltpu.SemaphoreType.DMA((PIECES,)),
            pltpu.SemaphoreType.DMA((PIECES,)),
            pltpu.SemaphoreType.DMA((PIECES,)),
            pltpu.SemaphoreType.DMA((PIECES,)),
            pltpu.SemaphoreType.DMA((2,)),
            pltpu.SemaphoreType.DMA((2,)),
        ],
        compiler_params=pltpu.CompilerParams(
            collective_id=0, has_side_effects=True, vmem_limit_bytes=60 * 2**20
        ),
    )
    weights = x_weights()

    def per_device(fields):
        tiles = fields.reshape(4, PLANES, ROWS // 8, 8, NX // 128, 128).transpose(0, 1, 2, 4, 3, 5)
        return call(tiles, jnp.asarray(weights))

    return jax.shard_map(
        per_device, mesh=mesh, in_specs=(placed,), out_specs=placed, check_vma=False
    )
```

```python
import functools

import jax
import jax.numpy as jnp
import numpy as np
from jax import lax
from jax.experimental import pallas as pl
from jax.experimental.pallas import tpu as pltpu
from jax.sharding import PartitionSpec as P

MESH = pl.DeviceIdType.MESH
F32, BF16 = jnp.float32, jnp.bfloat16
PAIRS = ((0, 0), (1, 1), (0, 1), (0, 2), (1, 3))
PRODUCTS = (0, 1, 4, 5, 8, 2, 3, 9, 6, 7)
PLANES, ROWS, NX = 3, 64, 4096
BLOCKS = 4
PIECES = 2 * PLANES
STEPS = PIECES * BLOCKS
SEND_AT, MID_AT, LAST_AT = 4, 14, 27


def gauss():
    t = np.arange(-16, 17).astype(np.float64)
    e = np.exp(-6.0 * t * t / 256.0)
    return e / e.sum()


G = [float(v) for v in gauss()[16:]]


def x_weights():
    g = gauss()
    w = np.zeros((1280, 128), np.float64)

    def put(row, x, col, coarse):
        t = x - 8 * coarse
        if abs(t) <= 16:
            w[row, col] = g[t + 16]

    for x in range(1024):
        for c in range(128):
            put(x, x, c, c)
    for x in range(128):
        put(1024 + x, x, 126, -2)
        put(1024 + x, x, 127, -1)
        put(1152 + x, 896 + x, 0, 128)
        put(1152 + x, 896 + x, 1, 129)
    w = w.astype(np.float32)
    high = w.astype(jnp.bfloat16)
    low = (w - high.astype(np.float32)).astype(jnp.bfloat16)
    return np.concatenate([high, low], axis=1)


def z_stage(load, row):
    acc = {}

    def add(key, value):
        acc[key] = value if key not in acc else acc[key] + value

    for b in (1, 2, 3):
        near = [load(f, b) for f in range(4)]
        far = [load(f, 8 - b) for f in range(4)]
        for p, (i, j) in enumerate(PAIRS):
            x, y = near[i] * near[j], far[i] * far[j]
            plus, minus = x + y, x - y
            add((p, 0), plus * ((G[b] + G[8 - b]) / 2))
            add((p, 1), minus * ((G[b] - G[8 - b]) / 2))
            add((p, 2), plus * ((G[8 + b] + G[16 - b]) / 2))
            add((p, 3), minus * ((G[8 + b] - G[16 - b]) / 2))
    four = [load(f, 4) for f in range(4)]
    zero = [load(f, 0) for f in range(4)]
    low_half = row < 4
    ends = (row == 0) | (row == 7)
    four_ends = (row < 2) | (row > 5)
    out = []
    for p, (i, j) in enumerate(PAIRS):
        r4, r0 = four[i] * four[j], zero[i] * zero[j]
        r8, r16 = r0 * G[8], r0 * G[16]
        d0, d1 = acc[p, 0] + r4 * G[4], acc[p, 2] + r4 * G[12]
        e0, e1 = acc[p, 1], acc[p, 3]
        s0, down1 = (d0 + e0) + r0 * G[0], (d0 - e0) + r8
        up1, down2 = (d1 + e1) + r8, (d1 - e1) + r16
        u1, u2 = pltpu.roll(up1, 7, 0), pltpu.roll(r16, 6, 0)
        v1, v2 = pltpu.roll(down1, 1, 0), pltpu.roll(down2, 2, 0)
        t1, t2 = jnp.where(low_half, v1, u1), jnp.where(low_half, v2, u2)
        w1, w2 = jnp.where(ends, t1, 0.0), jnp.where(four_ends, t2, 0.0)
        out.append((s0 + ((u1 + v1) - w1) + ((u2 + v2) - w2), t2 + w1))
    return out


def far_first(n):
    return sorted(range(1, n), key=lambda k: -min(k, n - k))


def turn(x, shift):
    shift %= 128
    return pltpu.roll(x, shift, 1) if shift else x


def kernel(
    sizes, f_hbm, w_hbm, o_ref, fields, w_ref, held, main_x, leak_x, sent1, got1, sent2, got2, whole, beside,
    f_sem, w_sem, s1_sem, r1_sem, s2_sem, r2_sem, sy_sem, ry_sem,
):
    n_xp, n_zp, n_gy = sizes
    xp, zp, gy = lax.axis_index("xp"), lax.axis_index("zp"), lax.axis_index("gy")
    has_prev, has_next = gy > 0, gy < n_gy - 1

    def fetch(unit):
        x_tiles = pl.ds(pl.multiple_of(lax.rem(unit, BLOCKS) * 8, 8), 8)
        plane = lax.rem(2 * (unit // BLOCKS), 3)
        return pltpu.make_async_copy(
            f_hbm.at[:, plane, :, x_tiles],
            fields.at[unit].reshape(4, 8, 9, 8, 128).at[:, :, pl.ds(0, 8)],
            f_sem.at[unit],
        )

    weights = pltpu.make_async_copy(w_hbm, w_ref, w_sem)
    weights.start()
    for unit in range(PLANES * BLOCKS):
        fetch(unit).start()

    barrier = pltpu.get_barrier_semaphore()

    def greet(**where):
        pl.semaphore_signal(barrier, inc=1, device_id=where, device_id_type=MESH)

    for k in range(1, n_zp):
        greet(zp=lax.rem(zp + k, n_zp))
    for k in range(1, n_xp):
        greet(xp=lax.rem(xp + k, n_xp))

    @pl.when(has_prev)
    def _():
        greet(gy=gy - 1)

    @pl.when(has_next)
    def _():
        greet(gy=gy + 1)

    def meet():
        beside_it = has_prev.astype(jnp.int32) + has_next.astype(jnp.int32)
        pl.semaphore_wait(barrier, n_xp + n_zp - 2 + beside_it)

    @pl.when(jnp.logical_not(has_prev))
    def _():
        beside[0] = jnp.zeros(beside.shape[1:], F32)

    @pl.when(jnp.logical_not(has_next))
    def _():
        beside[1] = jnp.zeros(beside.shape[1:], F32)

    row = lax.broadcasted_iota(jnp.int32, (8, 128), 0)
    lane = lax.broadcasted_iota(jnp.int32, (8, 128), 1)
    lane64 = lax.broadcasted_iota(jnp.int32, (64, 128), 1)
    def filter_z(step, h):
        piece, block = step // BLOCKS, lax.rem(step, BLOCKS)
        slot = lax.rem(step, 2)
        unit = (piece // 2) * BLOCKS + block
        half = lax.rem(piece, 2)
        names = (2 * half, 1 + 2 * half, 2 - half, 3 - 3 * half)

        def load(f, b):
            return fields[unit, pl.ds(names[f] * 576 + h * 8 + b, 8, stride=72), :]

        rows = z_stage(load, row)
        four_ends = (row < 2) | (row > 5)
        groups = [main for main, _ in rows]
        for a in (0, 2):
            groups.append(jnp.where(four_ends, rows[a][1], pltpu.roll(rows[a + 1][1], 4, 0)))
        groups.append(jnp.where(four_ends, rows[4][1], 0.0))
        for k in range(4):
            both = jnp.concatenate(groups[2 * k : 2 * k + 2], axis=0)
            high = both.astype(BF16)
            held[slot, h, 0, k] = high
            held[slot, h, 1, k] = (both - high.astype(F32)).astype(BF16)

    def filter_x(step):
        block, slot = lax.rem(step, BLOCKS), lax.rem(step, 2)
        cells = [held[slot, h].reshape(128, 128) for h in range(8)]

        def product(values, weight):
            r = jnp.dot(values, weight, preferred_element_type=F32)
            return r[:64, :128] + r[64:, :128] + r[:64, 128:]

        main_x[block] = product(jnp.concatenate(cells, axis=1), w_ref[0:1024])
        leak_x[block] = product(jnp.concatenate([cells[0], cells[7]], axis=1), w_ref[1024:1280])

    def transpose(piece, pair):
        both = []
        for block in (2 * pair, 2 * pair + 1):
            before, after = leak_x[(block + 3) % BLOCKS], leak_x[(block + 1) % BLOCKS]
            both.append(main_x[block] + jnp.where(lane64 < 2, before, jnp.where(lane64 > 125, after, 0.0)))
        y = jnp.transpose(jnp.concatenate(both, axis=0))
        for k in range(2):
            sent1[piece, :, 2 * pair + k] = y[64 * k : 64 * k + 64].reshape(8, 8, 128)

    def copy1(piece, to):
        return pltpu.make_async_remote_copy(
            src_ref=sent1.at[piece, to],
            dst_ref=got1.at[piece, zp],
            send_sem=s1_sem.at[piece],
            recv_sem=r1_sem.at[piece],
            device_id={"zp": to},
            device_id_type=MESH,
        )

    def copy2(piece, to):
        return pltpu.make_async_remote_copy(
            src_ref=sent2.at[piece, to],
            dst_ref=got2.at[piece, xp],
            send_sem=s2_sem.at[piece],
            recv_sem=r2_sem.at[piece],
            device_id={"xp": to},
            device_id_type=MESH,
        )

    def all1(piece):
        return pltpu.make_async_remote_copy(
            src_ref=sent1.at[piece, pl.ds(0, n_zp - 1)],
            dst_ref=got1.at[piece, pl.ds(0, n_zp - 1)],
            send_sem=s1_sem.at[piece],
            recv_sem=r1_sem.at[piece],
            device_id={"zp": lax.rem(zp + 1, n_zp)},
            device_id_type=MESH,
        )

    def all2(piece):
        return pltpu.make_async_remote_copy(
            src_ref=sent2.at[piece, pl.ds(0, n_xp - 1)],
            dst_ref=got2.at[piece, pl.ds(0, n_xp - 1)],
            send_sem=s2_sem.at[piece],
            recv_sem=r2_sem.at[piece],
            device_id={"xp": lax.rem(xp + 1, n_xp)},
            device_id_type=MESH,
        )

    def y_copy(side):
        return pltpu.make_async_remote_copy(
            src_ref=whole.at[1 - side],
            dst_ref=beside.at[side],
            send_sem=sy_sem.at[side],
            recv_sem=ry_sem.at[side],
            device_id={"gy": gy + 1 - 2 * side},
            device_id_type=MESH,
        )

    def start(side):
        @pl.when(has_next if side == 0 else has_prev)
        def _():
            y_copy(side).start()

    def send1(piece):
        for k in far_first(n_zp):
            copy1(piece, lax.rem(zp + k, n_zp)).start()
        got1[piece, zp] = sent1[piece, zp]

    def send2(piece, to):
        @pl.when(xp != to)
        def _():
            copy2(piece, to).start()

        @pl.when(xp == to)
        def _():
            got2[piece, to] = sent2[piece, to]

    group, within = lane // 8, lax.rem(lane, 8)
    outer = (lane < 2) | (lane > 125) | ((lane > 61) & (lane < 66))
    left = lane < 64
    first_two = lax.rem(lane, 4) < 2

    def middle(piece, block):
        v = [turn(got1[piece, k, block], 8 * k) for k in range(8)]
        yield
        for s in (1, 2, 4):
            bit = (group & s) == 0
            v = [jnp.where(bit, v[k], v[(k + s) % 8]) for k in range(8)]
        yield
        v = [v[-j % 8] for j in range(8)]
        out = None
        for j in range(5):
            e, back, shift = v[5 + j // 2], -8 * (5 + j // 2), 8 if j % 2 == 0 else 4
            up, down = turn(e, back + shift), turn(e, back - shift)
            z = jnp.where(within < 2, up, jnp.where(within > 5, down, 0.0))
            v[j] = turn(v[j], -8 * j) + jnp.where(outer, 0.0, z)
            z = turn(jnp.where(outer, z, 0.0), 4 * j + 2)
            out = z if out is None else out + z
        yield
        to = 4 * (block // 2) + block % 2
        for k in range(3):
            x, y = v[2 * k], v[2 * k + 1] if k < 2 else out
            swap = turn(jnp.where(left, y, x), 64)
            if k < 2:
                low, high = swap, y
            else:
                low, high = jnp.where(first_two, swap, y), jnp.where(first_two, y, swap)
            sent2[piece, to, k] = jnp.where(left, x, low)
            sent2[piece, to + 2, k] = jnp.where(left, swap, high)

    def last(piece):
        all2(piece).wait_recv()
        plane, half = piece // 2, lax.rem(piece, 2)
        e = [got2[piece, d, 2] for d in range(8)]
        around = []
        for g in range(4):
            near = jnp.where(first_two, e[2 * g + 1], e[2 * g])
            far = jnp.where(first_two, e[(2 * g + 2) % 8], e[(2 * g + 7) % 8])
            around.append(jnp.where(left, turn(far, 64), near))
        for j in range(5):
            for g in range(4):
                a, b = got2[piece, 2 * g, j // 2], got2[piece, 2 * g + 1, j // 2]
                main = jnp.where(left, a, turn(b, 64)) if j % 2 == 0 else jnp.where(left, turn(a, 64), b)
                z = turn(around[g], -2 - 4 * j)
                whole[plane, half * 5 + j, :, pl.ds(g * 128, 128)] = main + jnp.where(outer, z, 0.0)

    third = F32(1 / 3)
    scale0 = jnp.where(has_prev, third, F32(1 / 2))
    scale2 = jnp.where(has_next, third, F32(1 / 2))

    def box(half):
        for q in range(5 * half, 5 * half + 5):
            p, m0, m2, m1 = PRODUCTS[q], whole[0, q], whole[1, q], whole[2, q]
            o_ref[p, 0] = (m0 + m1 + beside[0, q]) * scale0
            o_ref[p, 1] = (m0 + m1 + m2) * third
            o_ref[p, 2] = (m1 + m2 + beside[1, q]) * scale2

    def one_step(step, carry):
        block = lax.rem(step, BLOCKS)

        @pl.when((step < STEPS) & (lax.rem(step, 2 * BLOCKS) < BLOCKS))
        def _():
            fetch((step // (2 * BLOCKS)) * BLOCKS + block).wait()

        @pl.when(step == 0)
        def _():
            weights.wait()

        @pl.when(step < STEPS)
        def _():
            filter_x(step + STEPS - 1)
            for h in range(8):
                filter_z(step, h)

        @pl.when(step == STEPS)
        def _():
            filter_x(step - 1)

        @pl.when(step == SEND_AT)
        def _():
            meet()

        @pl.when((block == SEND_AT % BLOCKS) & (step >= SEND_AT) & (step <= STEPS))
        def _():
            piece = (step - SEND_AT) // BLOCKS
            transpose(piece, 0)
            transpose(piece, 1)
            send1(piece)

        @pl.when((block == MID_AT % BLOCKS) & (step >= MID_AT) & (step < MID_AT + PIECES * BLOCKS))
        def _():
            piece = (step - MID_AT) // BLOCKS
            all1(piece).wait_recv()
            for pair in (0, 2):
                work = [middle(piece, pair), middle(piece, pair + 1)]
                while work:
                    work = [part for part in work if next(part, work) is not work]
                for to in range(2 * pair, 2 * pair + 4):
                    send2(piece, to)

        @pl.when((step == LAST_AT) | (step == LAST_AT + BLOCKS) | (step >= LAST_AT + 2 * BLOCKS))
        def _():
            last(jnp.where(step > LAST_AT + BLOCKS, step - LAST_AT - 2 * BLOCKS + 2, (step - LAST_AT) // BLOCKS))

        @pl.when(step == LAST_AT + BLOCKS)
        def _():
            start(1)

        @pl.when(step == LAST_AT + 2 * BLOCKS + 1)
        def _():
            start(0)

        return carry

    lax.fori_loop(0, LAST_AT + 2 * BLOCKS + 3, one_step, 0)
    last(PIECES - 1)
    for side in (0, 1):

        @pl.when(has_prev if side == 0 else has_next)
        def _():
            y_copy(side).wait_recv()

    box(0)
    box(1)

    for piece in range(PIECES):
        all1(piece).wait_send()
        all2(piece).wait_send()
    for side in (0, 1):

        @pl.when(has_next if side == 0 else has_prev)
        def _():
            y_copy(side).wait_send()


def solution(mesh):
    placed = P(None, "gy", ("xp", "zp"), None)
    sizes = tuple(mesh.shape[name] for name in ("xp", "zp", "gy"))
    call = pl.pallas_call(
        functools.partial(kernel, sizes),
        out_shape=pltpu.VMEM((10, PLANES, 8, 512), F32),
        in_specs=[pl.BlockSpec(memory_space=pl.ANY)] * 2,
        out_specs=pl.BlockSpec(memory_space=pltpu.VMEM),
        scratch_shapes=[
            pltpu.VMEM((PLANES * BLOCKS, 4 * ROWS * 9, 128), F32),
            pltpu.VMEM((1280, 256), BF16),
            pltpu.VMEM((2, 8, 2, 4, 16, 128), BF16),
            pltpu.VMEM((BLOCKS, 64, 128), F32),
            pltpu.VMEM((BLOCKS, 64, 128), F32),
            pltpu.VMEM((PIECES, 8, BLOCKS, 8, 128), F32),
            pltpu.VMEM((PIECES, 8, BLOCKS, 8, 128), F32),
            pltpu.VMEM((PIECES, 8, 3, 8, 128), F32),
            pltpu.VMEM((PIECES, 8, 3, 8, 128), F32),
            pltpu.VMEM((PLANES, 10, 8, 512), F32),
            pltpu.VMEM((2, 10, 8, 512), F32),
            pltpu.SemaphoreType.DMA((PLANES * BLOCKS,)),
            pltpu.SemaphoreType.DMA,
            pltpu.SemaphoreType.DMA((PIECES,)),
            pltpu.SemaphoreType.DMA((PIECES,)),
            pltpu.SemaphoreType.DMA((PIECES,)),
            pltpu.SemaphoreType.DMA((PIECES,)),
            pltpu.SemaphoreType.DMA((2,)),
            pltpu.SemaphoreType.DMA((2,)),
        ],
        compiler_params=pltpu.CompilerParams(
            collective_id=0, has_side_effects=True, vmem_limit_bytes=60 * 2**20
        ),
    )
    weights = x_weights()

    def per_device(fields):
        tiles = fields.reshape(4, PLANES, ROWS // 8, 8, NX // 128, 128).transpose(0, 1, 2, 4, 3, 5)
        return call(tiles, jnp.asarray(weights))

    return jax.shard_map(
        per_device, mesh=mesh, in_specs=(placed,), out_specs=placed, check_vma=False
    )
```

```python
import functools

import jax
import jax.numpy as jnp
import numpy as np
from jax import lax
from jax.experimental import pallas as pl
from jax.experimental.pallas import tpu as pltpu
from jax.sharding import PartitionSpec as P

MESH = pl.DeviceIdType.MESH
F32, BF16 = jnp.float32, jnp.bfloat16
PAIRS = ((0, 0), (1, 1), (0, 1), (0, 2), (1, 3))
PRODUCTS = (0, 1, 4, 5, 8, 2, 3, 9, 6, 7)
PLANES, ROWS, NX = 3, 64, 4096
BLOCKS = 4
PIECES = 2 * PLANES
STEPS = PIECES * BLOCKS
SEND_AT, MID_AT, LAST_AT = 4, 14, 27


def gauss():
    t = np.arange(-16, 17).astype(np.float64)
    e = np.exp(-6.0 * t * t / 256.0)
    return e / e.sum()


G = [float(v) for v in gauss()[16:]]


def x_weights():
    g = gauss()
    w = np.zeros((1280, 128), np.float64)

    def put(row, x, col, coarse):
        t = x - 8 * coarse
        if abs(t) <= 16:
            w[row, col] = g[t + 16]

    for x in range(1024):
        for c in range(128):
            put(x, x, c, c)
    for x in range(128):
        put(1024 + x, x, 126, -2)
        put(1024 + x, x, 127, -1)
        put(1152 + x, 896 + x, 0, 128)
        put(1152 + x, 896 + x, 1, 129)
    w = w.astype(np.float32)
    high = w.astype(jnp.bfloat16)
    low = (w - high.astype(np.float32)).astype(jnp.bfloat16)
    return np.concatenate([high, low], axis=1)


def z_stage(load, row):
    acc = {}

    def add(key, value):
        acc[key] = value if key not in acc else acc[key] + value

    for b in (1, 2, 3):
        near = [load(f, b) for f in range(4)]
        far = [load(f, 8 - b) for f in range(4)]
        for p, (i, j) in enumerate(PAIRS):
            x, y = near[i] * near[j], far[i] * far[j]
            plus, minus = x + y, x - y
            add((p, 0), plus * ((G[b] + G[8 - b]) / 2))
            add((p, 1), minus * ((G[b] - G[8 - b]) / 2))
            add((p, 2), plus * ((G[8 + b] + G[16 - b]) / 2))
            add((p, 3), minus * ((G[8 + b] - G[16 - b]) / 2))
    four = [load(f, 4) for f in range(4)]
    zero = [load(f, 0) for f in range(4)]
    low_half = row < 4
    ends = (row == 0) | (row == 7)
    four_ends = (row < 2) | (row > 5)
    out = []
    for p, (i, j) in enumerate(PAIRS):
        r4, r0 = four[i] * four[j], zero[i] * zero[j]
        r8, r16 = r0 * G[8], r0 * G[16]
        d0, d1 = acc[p, 0] + r4 * G[4], acc[p, 2] + r4 * G[12]
        e0, e1 = acc[p, 1], acc[p, 3]
        s0, down1 = (d0 + e0) + r0 * G[0], (d0 - e0) + r8
        up1, down2 = (d1 + e1) + r8, (d1 - e1) + r16
        u1, u2 = pltpu.roll(up1, 7, 0), pltpu.roll(r16, 6, 0)
        v1, v2 = pltpu.roll(down1, 1, 0), pltpu.roll(down2, 2, 0)
        t1, t2 = jnp.where(low_half, v1, u1), jnp.where(low_half, v2, u2)
        w1, w2 = jnp.where(ends, t1, 0.0), jnp.where(four_ends, t2, 0.0)
        out.append((s0 + ((u1 + v1) - w1) + ((u2 + v2) - w2), t2 + w1))
    return out


def far_first(n):
    return sorted(range(1, n), key=lambda k: -min(k, n - k))


def turn(x, shift):
    shift %= 128
    return pltpu.roll(x, shift, 1) if shift else x


def kernel(
    sizes, f_hbm, w_hbm, o_ref, fields, w_ref, held, main_x, leak_x, sent1, got1, sent2, got2, whole, beside,
    f_sem, w_sem, s1_sem, r1_sem, s2_sem, r2_sem, sy_sem, ry_sem,
):
    n_xp, n_zp, n_gy = sizes
    xp, zp, gy = lax.axis_index("xp"), lax.axis_index("zp"), lax.axis_index("gy")
    has_prev, has_next = gy > 0, gy < n_gy - 1

    def fetch(unit):
        x_tiles = pl.ds(pl.multiple_of(lax.rem(unit, BLOCKS) * 8, 8), 8)
        plane = lax.rem(2 * (unit // BLOCKS), 3)
        return pltpu.make_async_copy(
            f_hbm.at[:, plane, :, x_tiles],
            fields.at[unit].reshape(4, 8, 9, 8, 128).at[:, :, pl.ds(0, 8)],
            f_sem.at[unit],
        )

    weights = pltpu.make_async_copy(w_hbm, w_ref, w_sem)
    weights.start()
    for unit in range(PLANES * BLOCKS):
        fetch(unit).start()

    barrier = pltpu.get_barrier_semaphore()

    def greet(**where):
        pl.semaphore_signal(barrier, inc=1, device_id=where, device_id_type=MESH)

    for k in range(1, n_zp):
        greet(zp=lax.rem(zp + k, n_zp))
    for k in range(1, n_xp):
        greet(xp=lax.rem(xp + k, n_xp))

    @pl.when(has_prev)
    def _():
        greet(gy=gy - 1)

    @pl.when(has_next)
    def _():
        greet(gy=gy + 1)

    def meet():
        beside_it = has_prev.astype(jnp.int32) + has_next.astype(jnp.int32)
        pl.semaphore_wait(barrier, n_xp + n_zp - 2 + beside_it)

    @pl.when(jnp.logical_not(has_prev))
    def _():
        beside[0] = jnp.zeros(beside.shape[1:], F32)

    @pl.when(jnp.logical_not(has_next))
    def _():
        beside[1] = jnp.zeros(beside.shape[1:], F32)

    row = lax.broadcasted_iota(jnp.int32, (8, 128), 0)
    lane = lax.broadcasted_iota(jnp.int32, (8, 128), 1)
    lane64 = lax.broadcasted_iota(jnp.int32, (64, 128), 1)
    def filter_z(step, h):
        piece, block = step // BLOCKS, lax.rem(step, BLOCKS)
        slot = lax.rem(step, 2)
        unit = (piece // 2) * BLOCKS + block
        half = lax.rem(piece, 2)
        names = (2 * half, 1 + 2 * half, 2 - half, 3 - 3 * half)

        def load(f, b):
            return fields[unit, pl.ds(names[f] * 576 + h * 8 + b, 8, stride=72), :]

        rows = z_stage(load, row)
        four_ends = (row < 2) | (row > 5)
        groups = [main for main, _ in rows]
        for a in (0, 2):
            groups.append(jnp.where(four_ends, rows[a][1], pltpu.roll(rows[a + 1][1], 4, 0)))
        groups.append(jnp.where(four_ends, rows[4][1], 0.0))
        for k in range(4):
            both = jnp.concatenate(groups[2 * k : 2 * k + 2], axis=0)
            high = both.astype(BF16)
            held[slot, h, 0, k] = high
            held[slot, h, 1, k] = (both - high.astype(F32)).astype(BF16)

    def filter_x(step):
        block, slot = lax.rem(step, BLOCKS), lax.rem(step, 2)
        cells = [held[slot, h].reshape(128, 128) for h in range(8)]

        def product(values, weight):
            r = jnp.dot(values, weight, preferred_element_type=F32)
            return r[:64, :128] + r[64:, :128] + r[:64, 128:]

        main_x[block] = product(jnp.concatenate(cells, axis=1), w_ref[0:1024])
        leak_x[block] = product(jnp.concatenate([cells[0], cells[7]], axis=1), w_ref[1024:1280])

    def transpose(piece, pair):
        both = []
        for block in (2 * pair, 2 * pair + 1):
            before, after = leak_x[(block + 3) % BLOCKS], leak_x[(block + 1) % BLOCKS]
            both.append(main_x[block] + jnp.where(lane64 < 2, before, jnp.where(lane64 > 125, after, 0.0)))
        y = jnp.transpose(jnp.concatenate(both, axis=0))
        for k in range(2):
            sent1[piece, :, 2 * pair + k] = y[64 * k : 64 * k + 64].reshape(8, 8, 128)

    def copy1(piece, to):
        return pltpu.make_async_remote_copy(
            src_ref=sent1.at[piece, to],
            dst_ref=got1.at[piece, zp],
            send_sem=s1_sem.at[piece],
            recv_sem=r1_sem.at[piece],
            device_id={"zp": to},
            device_id_type=MESH,
        )

    def copy2(piece, to):
        return pltpu.make_async_remote_copy(
            src_ref=sent2.at[piece, to],
            dst_ref=got2.at[piece, xp],
            send_sem=s2_sem.at[piece],
            recv_sem=r2_sem.at[piece],
            device_id={"xp": to},
            device_id_type=MESH,
        )

    def all1(piece):
        return pltpu.make_async_remote_copy(
            src_ref=sent1.at[piece, pl.ds(0, n_zp - 1)],
            dst_ref=got1.at[piece, pl.ds(0, n_zp - 1)],
            send_sem=s1_sem.at[piece],
            recv_sem=r1_sem.at[piece],
            device_id={"zp": lax.rem(zp + 1, n_zp)},
            device_id_type=MESH,
        )

    def all2(piece):
        return pltpu.make_async_remote_copy(
            src_ref=sent2.at[piece, pl.ds(0, n_xp - 1)],
            dst_ref=got2.at[piece, pl.ds(0, n_xp - 1)],
            send_sem=s2_sem.at[piece],
            recv_sem=r2_sem.at[piece],
            device_id={"xp": lax.rem(xp + 1, n_xp)},
            device_id_type=MESH,
        )

    def y_copy(side):
        return pltpu.make_async_remote_copy(
            src_ref=whole.at[1 - side],
            dst_ref=beside.at[side],
            send_sem=sy_sem.at[side],
            recv_sem=ry_sem.at[side],
            device_id={"gy": gy + 1 - 2 * side},
            device_id_type=MESH,
        )

    def start(side):
        @pl.when(has_next if side == 0 else has_prev)
        def _():
            y_copy(side).start()

    def send1(piece):
        for k in far_first(n_zp):
            copy1(piece, lax.rem(zp + k, n_zp)).start()
        got1[piece, zp] = sent1[piece, zp]

    def send2(piece):
        for k in far_first(n_xp):
            copy2(piece, lax.rem(xp + k, n_xp)).start()
        got2[piece, xp] = sent2[piece, xp]

    group, within = lane // 8, lax.rem(lane, 8)
    outer = (lane < 2) | (lane > 125) | ((lane > 61) & (lane < 66))
    left = lane < 64
    first_two = lax.rem(lane, 4) < 2

    def middle(piece, block):
        v = [turn(got1[piece, k, block], 8 * k) for k in range(8)]
        yield
        for s in (1, 2, 4):
            bit = (group & s) == 0
            v = [jnp.where(bit, v[k], v[(k + s) % 8]) for k in range(8)]
        yield
        v = [v[-j % 8] for j in range(8)]
        out = None
        for j in range(5):
            e, back, shift = v[5 + j // 2], -8 * (5 + j // 2), 8 if j % 2 == 0 else 4
            up, down = turn(e, back + shift), turn(e, back - shift)
            z = jnp.where(within < 2, up, jnp.where(within > 5, down, 0.0))
            v[j] = turn(v[j], -8 * j) + jnp.where(outer, 0.0, z)
            z = turn(jnp.where(outer, z, 0.0), 4 * j + 2)
            out = z if out is None else out + z
        yield
        to = 4 * (block // 2) + block % 2
        for k in range(3):
            x, y = v[2 * k], v[2 * k + 1] if k < 2 else out
            swap = turn(jnp.where(left, y, x), 64)
            if k < 2:
                low, high = swap, y
            else:
                low, high = jnp.where(first_two, swap, y), jnp.where(first_two, y, swap)
            sent2[piece, to, k] = jnp.where(left, x, low)
            sent2[piece, to + 2, k] = jnp.where(left, swap, high)

    def last(piece):
        all2(piece).wait_recv()
        plane, half = piece // 2, lax.rem(piece, 2)
        e = [got2[piece, d, 2] for d in range(8)]
        around = []
        for g in range(4):
            near = jnp.where(first_two, e[2 * g + 1], e[2 * g])
            far = jnp.where(first_two, e[(2 * g + 2) % 8], e[(2 * g + 7) % 8])
            around.append(jnp.where(left, turn(far, 64), near))
        for j in range(5):
            for g in range(4):
                a, b = got2[piece, 2 * g, j // 2], got2[piece, 2 * g + 1, j // 2]
                main = jnp.where(left, a, turn(b, 64)) if j % 2 == 0 else jnp.where(left, turn(a, 64), b)
                z = turn(around[g], -2 - 4 * j)
                whole[plane, half * 5 + j, :, pl.ds(g * 128, 128)] = main + jnp.where(outer, z, 0.0)

    third = F32(1 / 3)
    scale0 = jnp.where(has_prev, third, F32(1 / 2))
    scale2 = jnp.where(has_next, third, F32(1 / 2))

    def box(half):
        for q in range(5 * half, 5 * half + 5):
            p, m0, m2, m1 = PRODUCTS[q], whole[0, q], whole[1, q], whole[2, q]
            o_ref[p, 0] = (m0 + m1 + beside[0, q]) * scale0
            o_ref[p, 1] = (m0 + m1 + m2) * third
            o_ref[p, 2] = (m1 + m2 + beside[1, q]) * scale2

    def one_step(step, carry):
        block = lax.rem(step, BLOCKS)

        @pl.when((step < STEPS) & (lax.rem(step, 2 * BLOCKS) < BLOCKS))
        def _():
            fetch((step // (2 * BLOCKS)) * BLOCKS + block).wait()

        @pl.when(step == 0)
        def _():
            weights.wait()

        @pl.when(step < STEPS)
        def _():
            filter_x(step + STEPS - 1)
            for h in range(8):
                filter_z(step, h)

        @pl.when(step == STEPS)
        def _():
            filter_x(step - 1)

        @pl.when(step == SEND_AT)
        def _():
            meet()

        @pl.when((block == SEND_AT % BLOCKS) & (step >= SEND_AT) & (step <= STEPS))
        def _():
            piece = (step - SEND_AT) // BLOCKS
            transpose(piece, 0)
            transpose(piece, 1)
            send1(piece)

        @pl.when((block == MID_AT % BLOCKS) & (step >= MID_AT) & (step < MID_AT + PIECES * BLOCKS))
        def _():
            piece = (step - MID_AT) // BLOCKS
            all1(piece).wait_recv()
            work = [middle(piece, part) for part in range(BLOCKS)]
            while work:
                work = [part for part in work if next(part, work) is not work]
            send2(piece)

        @pl.when((step == LAST_AT) | (step == LAST_AT + BLOCKS) | (step >= LAST_AT + 2 * BLOCKS))
        def _():
            last(jnp.where(step > LAST_AT + BLOCKS, step - LAST_AT - 2 * BLOCKS + 2, (step - LAST_AT) // BLOCKS))

        @pl.when(step == LAST_AT + BLOCKS)
        def _():
            start(1)

        @pl.when(step == LAST_AT + 2 * BLOCKS + 1)
        def _():
            start(0)

        return carry

    lax.fori_loop(0, LAST_AT + 2 * BLOCKS + 3, one_step, 0)
    last(PIECES - 1)
    for side in (0, 1):

        @pl.when(has_prev if side == 0 else has_next)
        def _():
            y_copy(side).wait_recv()

    box(0)
    box(1)

    for piece in range(PIECES):
        all1(piece).wait_send()
        all2(piece).wait_send()
    for side in (0, 1):

        @pl.when(has_next if side == 0 else has_prev)
        def _():
            y_copy(side).wait_send()


def solution(mesh):
    placed = P(None, "gy", ("xp", "zp"), None)
    sizes = tuple(mesh.shape[name] for name in ("xp", "zp", "gy"))
    call = pl.pallas_call(
        functools.partial(kernel, sizes),
        out_shape=pltpu.VMEM((10, PLANES, 8, 512), F32),
        in_specs=[pl.BlockSpec(memory_space=pl.ANY)] * 2,
        out_specs=pl.BlockSpec(memory_space=pltpu.VMEM),
        scratch_shapes=[
            pltpu.VMEM((PLANES * BLOCKS, 4 * ROWS * 9, 128), F32),
            pltpu.VMEM((1280, 256), BF16),
            pltpu.VMEM((2, 8, 2, 4, 16, 128), BF16),
            pltpu.VMEM((BLOCKS, 64, 128), F32),
            pltpu.VMEM((BLOCKS, 64, 128), F32),
            pltpu.VMEM((PIECES, 8, BLOCKS, 8, 128), F32),
            pltpu.VMEM((PIECES, 8, BLOCKS, 8, 128), F32),
            pltpu.VMEM((PIECES, 8, 3, 8, 128), F32),
            pltpu.VMEM((PIECES, 8, 3, 8, 128), F32),
            pltpu.VMEM((PLANES, 10, 8, 512), F32),
            pltpu.VMEM((2, 10, 8, 512), F32),
            pltpu.SemaphoreType.DMA((PLANES * BLOCKS,)),
            pltpu.SemaphoreType.DMA,
            pltpu.SemaphoreType.DMA((PIECES,)),
            pltpu.SemaphoreType.DMA((PIECES,)),
            pltpu.SemaphoreType.DMA((PIECES,)),
            pltpu.SemaphoreType.DMA((PIECES,)),
            pltpu.SemaphoreType.DMA((2,)),
            pltpu.SemaphoreType.DMA((2,)),
        ],
        compiler_params=pltpu.CompilerParams(
            collective_id=0, has_side_effects=True, vmem_limit_bytes=60 * 2**20
        ),
    )
    weights = x_weights()

    def per_device(fields):
        tiles = fields.reshape(4, PLANES, ROWS // 8, 8, NX // 128, 128).transpose(0, 1, 2, 4, 3, 5)
        return call(tiles, jnp.asarray(weights))

    return jax.shard_map(
        per_device, mesh=mesh, in_specs=(placed,), out_specs=placed, check_vma=False
    )
```
